512 devices in a mesh: depth: 8 (over y, core), row: 4 (over x), col: 16 (over z).
Axes of the slice: x: 4, y: 4, z: 16, core: 2. Of those that a mesh axis runs over, the one named last changes fastest.
Arguments:
- grad_out: bfloat16 [4096, 8192], P('depth', ('row', 'col')), may hold values from -16 to 16
- gate_pre: bfloat16 [4096, 14336], P('depth', ('row', 'col')), may hold values from -6 to 6
- up_pre: bfloat16 [4096, 14336], P('depth', ('row', 'col')), may hold values from -6 to 6
- down_weight: bfloat16 [14336, 8192], P(('row', 'col')), may hold values from -0.0625 to 0.0625
Outputs:
- grad_gate: bfloat16 [4096, 14336], P('depth', ('row', 'col'))
- grad_up: bfloat16 [4096, 14336], P('depth', ('row', 'col'))
- grad_down: bfloat16 [14336, 8192], P(('row', 'col'), 'depth')
The draws below stay inside these ranges and needn't reach their ends.
All inputs are finite; a program needn't handle non-finite values.
Results may differ from the reference program's by a relative error of at most 0.017.
Values may be sent and summed in bfloat16 or wider, within the bound.
No kernel may reach another device: no remote copies, remote signals or barrier semaphores. Data moves between devices by JAX's collectives and lax.ppermute only.
A program may use at most 64 MiB of HBM per device.

```python
import jax
import jax.numpy as jnp
from jax import lax

D = 8192
FF = 14336
TOK_DEV = 512
TOKENS = 4096
N_DEPTH = 8


def strengthened(array, key, source, target, parts, factor):
    owner, partner = [(jnp.arange(array.shape[axis_at]) // (array.shape[axis_at] // parts)).reshape([-1 if axis == axis_at else 1 for axis in range(array.ndim)]) for axis_at in (source, target)]
    chosen = jax.random.permutation(key, parts)[partner]
    strong = (owner == chosen) | (owner == (partner + parts // 2) % parts)
    return jnp.where(strong, factor * array, array)


def levels(key, dims, cuts, low, largest):
    gain, own = 1.0, jax.random.fold_in(key, 6)
    for position, parts in cuts:
        heights = jnp.exp(jax.random.uniform(jax.random.fold_in(own, position), (parts,), jnp.float32, low / len(cuts), largest / len(cuts)))
        gain = gain * jnp.repeat(heights, dims[position] // parts).reshape([-1 if axis == position else 1 for axis in range(len(dims))])
    return gain


def normal_values(key, shape, spread, reach, pieces=(), kind=jnp.bfloat16):
    entries = spread * jax.random.normal(key, shape, jnp.float32)
    if pieces:
        entries = entries * levels(key, shape, pieces, -0.22, 0.18)
    return jnp.clip(entries, -reach, reach).astype(kind)


def gaussian_with(key, dims, deviation, most, shards, heavy, dtype=jnp.bfloat16):
    array = deviation * jax.random.normal(key, dims, jnp.float32)
    if shards:
        array = array * levels(key, dims, shards, -0.22, 0.18)
    return jnp.clip(strengthened(array, jax.random.fold_in(key, 3), *heavy), -most, most).astype(dtype)


def setup_inputs(seed: int = 0) -> dict:
    splits = jax.random.split(jax.random.key(seed), 5)
    grad_out = gaussian_with(splits[0], (TOKENS, D), 1.0, 16.0, ((0, 8), (1, 64)), (0, 1, 64, 4.0))
    gate_pre = normal_values(splits[1], (TOKENS, FF), 1.5, 6.0, ((0, 8), (1, 64)))
    up_pre = normal_values(splits[2], (TOKENS, FF), 1.0, 6.0, ((0, 8), (1, 64)))
    down_weight = normal_values(splits[3], (FF, D), D ** -0.5, 0.0625, ((0, 64),))
    return dict(grad_out=grad_out, gate_pre=gate_pre, up_pre=up_pre, down_weight=down_weight)


def reference(grad_out, gate_pre, up_pre, down_weight):
    gate = gate_pre.astype(jnp.float32)
    upval = up_pre.astype(jnp.float32)
    sigma = jax.nn.sigmoid(gate)
    active = gate * sigma
    hidden = (active * upval).astype(jnp.bfloat16)
    grad_hidden = jnp.dot(grad_out, down_weight.T, preferred_element_type=jnp.float32)
    grad_up = (grad_hidden * active).astype(jnp.bfloat16)
    grad_gate = (grad_hidden * upval * sigma * (1.0 + gate * (1.0 - sigma))).astype(jnp.bfloat16)
    scale = 1.0 / jnp.sqrt(jnp.float32(TOKENS))
    hidden_groups = hidden.reshape(N_DEPTH, TOK_DEV, FF)
    grad_groups = grad_out.reshape(N_DEPTH, TOK_DEV, D)

    def accumulate(total, group):
        hid, grd = group
        term = lax.dot_general(hid, grd, (((0,), (0,)), ((), ())), preferred_element_type=jnp.float32)
        return (total + (term * scale).astype(jnp.bfloat16).astype(jnp.float32), None)
    total, _ = lax.scan(accumulate, jnp.zeros((FF, D), jnp.float32), (hidden_groups, grad_groups))
    return (grad_gate, grad_up, total.astype(jnp.bfloat16))
```

```python
import jax
import jax.numpy as jnp
from jax import lax
from jax.experimental import pallas as pl
from jax.experimental.pallas import tpu as pltpu
from jax.sharding import PartitionSpec as P

ZG = [[g + 4 * j for j in range(4)] for g in range(4)]
YS = [[0, 2, 4, 6], [1, 3, 5, 7]]


def from_col(a, k):
    return lax.ppermute(a, "col", [((i + k) % 16, i) for i in range(16)])


def other_core(a):
    return lax.ppermute(a, "depth", [(i, i ^ 1) for i in range(8)])


def wide(ref):
    return jnp.concatenate([ref[0], ref[1]], axis=1)


def partial_kernel(pos, hid, s0, s1, s2, s3, out):
    rows = hid.shape[0] * hid.shape[1]
    h = hid[...].reshape(rows, hid.shape[2])
    for r, s in enumerate((s0, s1, s2, s3)):
        p = jnp.dot(h, wide(s), preferred_element_type=jnp.float32) * (1.0 / 64.0)
        out[:, :, r * 256 : r * 256 + 256] = p.astype(out.dtype).reshape(hid.shape[0], hid.shape[1], 256)


def partial_add_kernel(pos, hid, s0, s1, s2, s3, got, out):
    rows = hid.shape[0] * hid.shape[1]
    h = hid[...].reshape(rows, hid.shape[2])
    for r, s in enumerate((s0, s1, s2, s3)):
        p = jnp.dot(h, wide(s), preferred_element_type=jnp.float32) * (1.0 / 64.0)
        q = p.reshape(hid.shape[0], hid.shape[1], 256) + got[:, :, r * 256 : r * 256 + 256].astype(jnp.float32)
        out[:, :, r * 256 : r * 256 + 256] = q.astype(out.dtype)


def partial_call(pos, which, hid, sets, got=None):
    n, f, t = hid.shape
    whole = lambda shape: pl.BlockSpec(shape, lambda i, p: (0,) * len(shape))
    half = pl.BlockSpec((2, t, 128), lambda i, p: (p[which], 0, 0))
    specs = [whole((n, f, t))] + [half] * 4 + ([whole((n, f, 1024))] if got is not None else [])
    args = [hid, *sets] + ([got] if got is not None else [])
    return pl.pallas_call(
        partial_kernel if got is None else partial_add_kernel,
        grid_spec=pltpu.PrefetchScalarGridSpec(
            num_scalar_prefetch=1, grid=(1,), in_specs=specs, out_specs=whole((n, f, 1024))
        ),
        out_shape=jax.ShapeDtypeStruct((n, f, 1024), jnp.bfloat16),
        compiler_params=pltpu.CompilerParams(vmem_limit_bytes=48 * 1024 * 1024),
        cost_estimate=pl.CostEstimate(flops=2 * n * f * t * 1024, bytes_accessed=4 * 1024 * 1024, transcendentals=0),
    )(pos, *args)


def hidden_grad_kernel(pos, wa, wb, a0, a1, a2, a3, b0, b1, b2, b3, out, acc, cat):
    i = pl.program_id(0)
    zl = pos[2]
    rows = wa.shape[0] * wa.shape[1]
    total = None
    for r in range(4):
        at = pl.multiple_of(lax.rem(zl + r, 4) * 128, 128)
        cat[0, :, pl.ds(at, 128)] = (a0, a1, a2, a3)[r][0]
        cat[1, :, pl.ds(at, 128)] = (b0, b1, b2, b3)[r][0]
    for k, w in enumerate((wa, wb)):
        part = lax.dot_general(
            w[...].reshape(rows, w.shape[2]), cat[k], (((1,), (1,)), ((), ())), preferred_element_type=jnp.float32
        )
        total = part if total is None else total + part

    @pl.when(i == 0)
    def _():
        acc[...] = total

    @pl.when(i == 1)
    def _():
        out[...] = (acc[...] + total).astype(out.dtype).reshape(out.shape)


def hidden_grad_call(pos, wa, wb, sets):
    n, f, _ = wa.shape
    t = sets[0].shape[1]
    wspec = pl.BlockSpec((n, f, 512), lambda i, p: (0, 0, i))
    mine = pl.BlockSpec((1, t, 128), lambda i, p: (2 * p[0] + i, 0, 0))
    others = pl.BlockSpec((1, t, 128), lambda i, p: (2 * p[1] + i, 0, 0))
    return pl.pallas_call(
        hidden_grad_kernel,
        grid_spec=pltpu.PrefetchScalarGridSpec(
            num_scalar_prefetch=1,
            grid=(2,),
            in_specs=[wspec, wspec] + [mine] * 4 + [others] * 4,
            out_specs=pl.BlockSpec((n, f, t), lambda i, p: (0, 0, 0)),
            scratch_shapes=[pltpu.VMEM((n * f, t), jnp.float32), pltpu.VMEM((2, t, 512), jnp.bfloat16)],
        ),
        out_shape=jax.ShapeDtypeStruct((n, f, t), jnp.bfloat16),
        compiler_params=pltpu.CompilerParams(vmem_limit_bytes=48 * 1024 * 1024),
        cost_estimate=pl.CostEstimate(flops=2 * n * f * t * 2048, bytes_accessed=7 * 1024 * 1024, transcendentals=0),
    )(pos, wa, wb, *sets, *sets)


def sum_kernel(pos, q, out):
    zl = pos[2]
    for r in range(4):
        for k in range(2):
            lo = r * 256 + k * 128
            s = q[0, :, lo : lo + 128].astype(jnp.float32)
            for y in range(1, 4):
                s = s + q[y, :, lo : lo + 128].astype(jnp.float32)
            at = pl.multiple_of(k * 512 + lax.rem(zl + r, 4) * 128, 128)
            out[:, pl.ds(at, 128)] = s.astype(out.dtype)


def sum_call(pos, q):
    n, f, d = q.shape
    return pl.pallas_call(
        sum_kernel,
        grid_spec=pltpu.PrefetchScalarGridSpec(
            num_scalar_prefetch=1,
            grid=(1,),
            in_specs=[pl.BlockSpec((n, f, d), lambda i, p: (0, 0, 0))],
            out_specs=pl.BlockSpec((f, d), lambda i, p: (0, 0)),
        ),
        out_shape=jax.ShapeDtypeStruct((f, d), jnp.bfloat16),
        compiler_params=pltpu.CompilerParams(vmem_limit_bytes=32 * 1024 * 1024),
        cost_estimate=pl.CostEstimate(flops=n * f * d, bytes_accessed=5 * f * d * 2, transcendentals=0),
    )(pos, q)


def shards(grad_out, gate_pre, up_pre, down_weight):
    depth, row, col = lax.axis_index("depth"), lax.axis_index("row"), lax.axis_index("col")
    core = depth % 2
    zl = col % 4
    pos = jnp.stack([core, 1 - core, zl]).astype(jnp.int32)
    f = down_weight.shape[0]

    gate = gate_pre.T.astype(jnp.float32)
    upval = up_pre.T.astype(jnp.float32)
    sigma = jax.nn.sigmoid(gate)
    active = gate * sigma
    hidden = (active * upval).astype(jnp.bfloat16)

    hid = lax.all_to_all(jnp.broadcast_to(hidden[None], (4,) + hidden.shape), "row", 0, 0)
    hid = lax.dynamic_slice_in_dim(jnp.concatenate([hid, hid]), (4 - row) % 4, 4, 0)

    wcols = lax.dynamic_index_in_dim(down_weight.reshape(f, 4, 2, 1024), core, 2, keepdims=False)
    wa = lax.all_to_all(wcols.transpose(1, 0, 2), "row", 0, 0)
    wb = other_core(wa)

    set0 = lax.all_gather(grad_out, "col", axis=0, axis_index_groups=ZG)
    set1 = from_col(set0, 1)
    set3 = from_col(set0, -1)
    set2 = jnp.concatenate([from_col(set0[:2], 2), from_col(set0[2:], -2)])
    sets = (set0, set1, set2, set3)

    away = partial_call(pos, 1, hid, sets)
    both = partial_call(pos, 0, hid, sets, other_core(away))
    parts = lax.all_to_all(both, "depth", 0, 0, axis_index_groups=YS)
    total = sum_call(pos, parts)
    perm = []
    for y in range(4):
        for c in range(2):
            for x in range(4):
                perm.append(((2 * y + c) * 4 + x, (2 * x + c) * 4 + (y - x) % 4))
    grad_down = lax.ppermute(total, ("depth", "row"), perm)

    terms = lax.all_to_all(hidden_grad_call(pos, wa, wb, sets), "row", 0, 0)
    grad_hidden = terms.astype(jnp.float32).sum(0)
    grad_up = (grad_hidden * active).astype(jnp.bfloat16)
    grad_gate = (grad_hidden * upval * sigma * (1.0 + gate * (1.0 - sigma))).astype(jnp.bfloat16)
    return (grad_gate.T, grad_up.T, grad_down)


def solution(mesh):
    in_specs = (
        P("depth", ("row", "col")),
        P("depth", ("row", "col")),
        P("depth", ("row", "col")),
        P(("row", "col"), None),
    )
    out_specs = (P("depth", ("row", "col")), P("depth", ("row", "col")), P(("row", "col"), "depth"))
    return jax.shard_map(shards, mesh=mesh, in_specs=in_specs, out_specs=out_specs, check_vma=False)
```

```python
import jax
import jax.numpy as jnp
from jax import lax
from jax.experimental import pallas as pl
from jax.experimental.pallas import tpu as pltpu
from jax.sharding import PartitionSpec as P

ZG = [[g + 4 * j for j in range(4)] for g in range(4)]

def from_col(a, k):
    return lax.ppermute(a, "col", [((i + k) % 16, i) for i in range(16)])


def other_core(a):
    return lax.ppermute(a, "depth", [(i, i ^ 1) for i in range(8)])


def columns_kernel(pos, *refs):
    for i in range(4):
        refs[4][i] = refs[i][...]


def columns_call(pos, w):
    f, d = w.shape
    return pl.pallas_call(
        columns_kernel,
        grid_spec=pltpu.PrefetchScalarGridSpec(
            num_scalar_prefetch=1,
            grid=(1,),
            in_specs=[pl.BlockSpec((f, d // 8), lambda g, p, i=i: (0, 2 * i + p[0])) for i in range(4)],
            out_specs=pl.BlockSpec((4, f, d // 8), lambda g, p: (0, 0, 0)),
        ),
        out_shape=jax.ShapeDtypeStruct((4, f, d // 8), jnp.bfloat16),
        compiler_params=pltpu.CompilerParams(vmem_limit_bytes=32 * 1024 * 1024),
        cost_estimate=pl.CostEstimate(flops=0, bytes_accessed=2 * f * d, transcendentals=0),
    )(pos, w, w, w, w)


def hidden_kernel(gate, up, after, out):
    g = gate[...].astype(jnp.float32)
    out[...] = (g * jax.nn.sigmoid(g) * up[...].astype(jnp.float32)).astype(out.dtype)


def hidden_call(gate, up, after):
    spec = pl.BlockSpec(gate.shape, lambda i: (0, 0))
    return pl.pallas_call(
        hidden_kernel,
        grid=(1,),
        in_specs=[spec, spec, pl.BlockSpec(memory_space=pl.ANY)],
        out_specs=spec,
        out_shape=jax.ShapeDtypeStruct(gate.shape, jnp.bfloat16),
        cost_estimate=pl.CostEstimate(flops=0, bytes_accessed=6 * gate.size, transcendentals=gate.size),
    )(gate, up, after)


def set_blocks(sets, halves):
    specs, args = [], []
    for h in halves:
        for s in sets:
            for q in range(2):
                if isinstance(s, tuple):
                    specs.append(pl.BlockSpec((1, 512, 128), lambda i, p, h=h: (p[h], 0, 0)))
                    args.append(s[q])
                else:
                    specs.append(pl.BlockSpec((1, 512, 128), lambda i, p, h=h, q=q: (2 * p[h] + q, 0, 0)))
                    args.append(s)
    return specs, args


def gather_features(pos, blocks, cat):
    for k in range(cat.shape[0]):
        for r in range(4):
            for q in range(2):
                at = pl.multiple_of(q * 512 + lax.rem(pos[2] + r, 4) * 128, 128)
                cat[k, :, pl.ds(at, 128)] = blocks[8 * k + 2 * r + q][0]


def partial_kernel(pos, *refs):
    cat = refs[-1]
    gather_features(pos, refs[4:12], cat)
    h = jnp.concatenate([refs[j][0] for j in range(4)], axis=0)
    p = jnp.dot(h, cat[0], preferred_element_type=jnp.float32) * (1.0 / 64.0)
    f = refs[0].shape[1]
    if len(refs) == 14:
        for j in range(4):
            refs[12][j] = p[j * f : j * f + f].astype(jnp.bfloat16)
    else:
        got, outs = refs[12], refs[13:17]
        for j in range(4):
            outs[j][...] = (p[j * f : j * f + f] + got[j].astype(jnp.float32)).astype(jnp.bfloat16)


def partial_call(pos, which, hid, sets, got=None):
    n, f, t = hid.shape
    specs, args = set_blocks(sets, (which,))
    rows = [pl.BlockSpec((1, f, t), lambda i, p, j=j: (lax.rem(p[4] + 4 + j - p[3], 4), 0, 0)) for j in range(4)]
    whole = pl.BlockSpec((n, f, 1024), lambda i, p: (0, 0, 0))
    one = pl.BlockSpec((f, 1024), lambda i, p: (0, 0))
    if got is None:
        out_specs, out_shape = whole, jax.ShapeDtypeStruct((n, f, 1024), jnp.bfloat16)
    else:
        out_specs, out_shape = [one] * 4, [jax.ShapeDtypeStruct((f, 1024), jnp.bfloat16)] * 4
        specs, args = specs + [whole], args + [got]
    return pl.pallas_call(
        partial_kernel,
        grid_spec=pltpu.PrefetchScalarGridSpec(
            num_scalar_prefetch=1,
            grid=(1,),
            in_specs=rows + specs,
            out_specs=out_specs,
            scratch_shapes=[pltpu.VMEM((1, t, 1024), jnp.bfloat16)],
        ),
        out_shape=out_shape,
        compiler_params=pltpu.CompilerParams(vmem_limit_bytes=48 * 1024 * 1024),
        cost_estimate=pl.CostEstimate(flops=2 * n * f * t * 1024, bytes_accessed=5 * 1024 * 1024, transcendentals=0),
    )(pos, hid, hid, hid, hid, *args)


def sum_kernel(a, b, c, d, out):
    total = a[...].astype(jnp.float32) + b[...].astype(jnp.float32)
    out[...] = (total + c[...].astype(jnp.float32) + d[...].astype(jnp.float32)).astype(out.dtype)


def sum_call(parts):
    f, d = parts[0].shape
    spec = pl.BlockSpec((f // 2, d), lambda i: (i, 0))
    return pl.pallas_call(
        sum_kernel,
        grid=(2,),
        in_specs=[spec] * 4,
        out_specs=spec,
        out_shape=jax.ShapeDtypeStruct((f, d), jnp.bfloat16),
        cost_estimate=pl.CostEstimate(flops=3 * f * d, bytes_accessed=10 * f * d, transcendentals=0),
    )(*parts)


def hidden_grad_kernel(pos, wa, wb, *refs):
    blocks, out, cat = refs[:16], refs[16], refs[17]
    n, f, d = wa.shape

    @pl.when(pl.program_id(0) == 0)
    def _():
        gather_features(pos, blocks, cat)

    total = None
    for k, w in enumerate((wa, wb)):
        part = lax.dot_general(
            w[...].reshape(n * f, d), cat[k], (((1,), (1,)), ((), ())), preferred_element_type=jnp.float32
        )
        total = part if total is None else total + part
    out[...] = total.astype(out.dtype).reshape(out.shape)


def hidden_grad_call(pos, wa, wb, sets):
    n, f, d = wa.shape
    t = 512
    specs, args = set_blocks(sets, (0, 1))
    wspec = pl.BlockSpec((2, f, d), lambda i, p: (i, 0, 0))
    return pl.pallas_call(
        hidden_grad_kernel,
        grid_spec=pltpu.PrefetchScalarGridSpec(
            num_scalar_prefetch=1,
            grid=(2,),
            in_specs=[wspec, wspec] + specs,
            out_specs=pl.BlockSpec((2, f, t), lambda i, p: (i, 0, 0)),
            scratch_shapes=[pltpu.VMEM((2, t, d), jnp.bfloat16)],
        ),
        out_shape=jax.ShapeDtypeStruct((n, f, t), jnp.bfloat16),
        compiler_params=pltpu.CompilerParams(vmem_limit_bytes=48 * 1024 * 1024),
        cost_estimate=pl.CostEstimate(flops=4 * n * f * t * d, bytes_accessed=7 * 1024 * 1024, transcendentals=0),
    )(pos, wa, wb, *args)


def shards(grad_out, gate_pre, up_pre, down_weight):
    depth, row, col = lax.axis_index("depth"), lax.axis_index("row"), lax.axis_index("col")
    pos = jnp.stack([depth % 2, 1 - depth % 2, col % 4, row, depth // 2]).astype(jnp.int32)

    wa = lax.all_to_all(columns_call(pos, down_weight), "row", 0, 0)
    wb = other_core(wa)

    set0 = lax.all_gather(grad_out, "col", axis=0, axis_index_groups=ZG)
    set2 = (from_col(set0[0::2], 2), from_col(set0[1::2], -2))
    set1 = from_col(set0, 1)
    set3 = from_col(set0, -1)
    sets = (set0, set1, set2, set3)

    hid = lax.all_gather(hidden_call(gate_pre.T, up_pre.T, set0), "row", axis=0)

    away = partial_call(pos, 1, hid, sets)
    both = partial_call(pos, 0, hid, sets, other_core(away))
    parts = [both[0]]
    for j in (1, 3, 2):
        parts.append(lax.ppermute(both[j], "depth", [(i, (i + 2 * j) % 8) for i in range(8)]))
    perm = []
    for y in range(4):
        for c in range(2):
            for x in range(4):
                perm.append(((2 * y + c) * 4 + x, (2 * x + c) * 4 + (y - x) % 4))
    grad_down = lax.ppermute(sum_call(parts), ("depth", "row"), perm)

    gate = gate_pre.T.astype(jnp.float32)
    upval = up_pre.T.astype(jnp.float32)
    sigma = jax.nn.sigmoid(gate)
    active = gate * sigma
    terms = lax.all_to_all(hidden_grad_call(pos, wa, wb, sets), "row", 0, 0)
    grad_hidden = terms.astype(jnp.float32).sum(0)
    grad_up = (grad_hidden * active).astype(jnp.bfloat16)
    grad_gate = (grad_hidden * upval * sigma * (1.0 + gate * (1.0 - sigma))).astype(jnp.bfloat16)
    return (grad_gate.T, grad_up.T, grad_down)


def solution(mesh):
    in_specs = (
        P("depth", ("row", "col")),
        P("depth", ("row", "col")),
        P("depth", ("row", "col")),
        P(("row", "col"), None),
    )
    out_specs = (P("depth", ("row", "col")), P("depth", ("row", "col")), P(("row", "col"), "depth"))
    return jax.shard_map(shards, mesh=mesh, in_specs=in_specs, out_specs=out_specs, check_vma=False)
```

```python
import jax
import jax.numpy as jnp
from jax import lax
from jax.experimental import pallas as pl
from jax.experimental.pallas import tpu as pltpu
from jax.sharding import PartitionSpec as P

ZG = [[g + 4 * j for j in range(4)] for g in range(4)]

def from_col(a, k):
    return lax.ppermute(a, "col", [((i + k) % 16, i) for i in range(16)])


def other_core(a):
    return lax.ppermute(a, "depth", [(i, i ^ 1) for i in range(8)])


def columns_kernel(pos, w, out, sems):
    d = out.shape[2]
    copies = [
        pltpu.make_async_copy(w.at[:, pl.ds(pl.multiple_of((2 * i + pos[0]) * d, d), d)], out.at[i], sems.at[i])
        for i in range(4)
    ]
    for c in copies:
        c.start()
    for c in copies:
        c.wait()


def columns_call(pos, w):
    f, d = w.shape
    return pl.pallas_call(
        columns_kernel,
        grid_spec=pltpu.PrefetchScalarGridSpec(
            num_scalar_prefetch=1,
            grid=(1,),
            in_specs=[pl.BlockSpec(memory_space=pltpu.HBM)],
            out_specs=pl.BlockSpec((4, f, d // 8), lambda g, p: (0, 0, 0)),
            scratch_shapes=[pltpu.SemaphoreType.DMA((4,))],
        ),
        out_shape=jax.ShapeDtypeStruct((4, f, d // 8), jnp.bfloat16),
        compiler_params=pltpu.CompilerParams(vmem_limit_bytes=12 * 1024 * 1024),
        cost_estimate=pl.CostEstimate(flops=0, bytes_accessed=2 * f * d, transcendentals=0),
    )(pos, w)


def hidden_kernel(gate, up, after, out):
    g = gate[...].astype(jnp.float32)
    out[...] = (g * jax.nn.sigmoid(g) * up[...].astype(jnp.float32)).astype(out.dtype)


def hidden_call(gate, up, after):
    spec = pl.BlockSpec(gate.shape, lambda i: (0, 0))
    return pl.pallas_call(
        hidden_kernel,
        grid=(1,),
        in_specs=[spec, spec, pl.BlockSpec(memory_space=pl.ANY)],
        out_specs=spec,
        out_shape=jax.ShapeDtypeStruct(gate.shape, jnp.bfloat16),
        compiler_params=pltpu.CompilerParams(vmem_limit_bytes=8 * 1024 * 1024),
        cost_estimate=pl.CostEstimate(flops=0, bytes_accessed=6 * gate.size, transcendentals=gate.size),
    )(gate, up, after)


def set_blocks(sets, halves):
    specs, args = [], []
    for h in halves:
        for s in sets:
            for q in range(2):
                if isinstance(s, tuple):
                    specs.append(pl.BlockSpec((1, 512, 128), lambda i, p, h=h: (p[h], 0, 0)))
                    args.append(s[q])
                else:
                    specs.append(pl.BlockSpec((1, 512, 128), lambda i, p, h=h, q=q: (2 * p[h] + q, 0, 0)))
                    args.append(s)
    return specs, args


def gather_features(pos, blocks, cat):
    for k in range(cat.shape[0]):
        for r in range(4):
            for q in range(2):
                at = pl.multiple_of(q * 512 + lax.rem(pos[2] + r, 4) * 128, 128)
                cat[k, :, pl.ds(at, 128)] = blocks[8 * k + 2 * r + q][0]


def partial_kernel(pos, *refs):
    cat = refs[-1]
    gather_features(pos, refs[4:12], cat)
    h = jnp.concatenate([refs[j][0] for j in range(4)], axis=0)
    p = jnp.dot(h, cat[0], preferred_element_type=jnp.float32) * (1.0 / 64.0)
    f = refs[0].shape[1]
    if len(refs) == 14:
        for j in range(4):
            refs[12][j] = p[j * f : j * f + f].astype(jnp.bfloat16)
    else:
        got, outs = refs[12], refs[13:17]
        for j in range(4):
            outs[j][...] = (p[j * f : j * f + f] + got[j].astype(jnp.float32)).astype(jnp.bfloat16)


def partial_call(pos, which, hid, sets, got=None):
    n, f, t = hid.shape
    specs, args = set_blocks(sets, (which,))
    rows = [pl.BlockSpec((1, f, t), lambda i, p, j=j: (lax.rem(p[4] + 4 + j - p[3], 4), 0, 0)) for j in range(4)]
    whole = pl.BlockSpec((n, f, 1024), lambda i, p: (0, 0, 0))
    kept = pl.BlockSpec(memory_space=pltpu.VMEM)
    if got is None:
        out_specs, out_shape = kept, pltpu.VMEM((n, f, 1024), jnp.bfloat16)
    else:
        out_specs, out_shape = [kept] * 4, [pltpu.VMEM((f, 1024), jnp.bfloat16)] * 4
        specs, args = specs + [whole], args + [got]
    return pl.pallas_call(
        partial_kernel,
        grid_spec=pltpu.PrefetchScalarGridSpec(
            num_scalar_prefetch=1,
            grid=(1,),
            in_specs=rows + specs,
            out_specs=out_specs,
            scratch_shapes=[pltpu.VMEM((1, t, 1024), jnp.bfloat16)],
        ),
        out_shape=out_shape,
        compiler_params=pltpu.CompilerParams(vmem_limit_bytes=18 * 1024 * 1024),
        cost_estimate=pl.CostEstimate(flops=2 * n * f * t * 1024, bytes_accessed=5 * 1024 * 1024, transcendentals=0),
    )(pos, hid, hid, hid, hid, *args)


def sum_kernel(a, b, c, d, after, out):
    total = a[...].astype(jnp.float32) + b[...].astype(jnp.float32)
    out[...] = (total + c[...].astype(jnp.float32) + d[...].astype(jnp.float32)).astype(out.dtype)


def sum_call(parts, after):
    f, d = parts[0].shape
    return pl.pallas_call(
        sum_kernel,
        in_specs=[pl.BlockSpec(memory_space=pltpu.VMEM)] * 4 + [pl.BlockSpec(memory_space=pl.ANY)],
        out_specs=pl.BlockSpec(memory_space=pltpu.VMEM),
        out_shape=pltpu.VMEM((f, d), jnp.bfloat16),
        compiler_params=pltpu.CompilerParams(vmem_limit_bytes=8 * 1024 * 1024),
        cost_estimate=pl.CostEstimate(flops=3 * f * d, bytes_accessed=10 * f * d, transcendentals=0),
    )(*parts, after)


def hidden_grad_kernel(pos, wa, wb, *refs):
    blocks, outs, cat = refs[:16], refs[16:20], refs[20]
    gather_features(pos, blocks, cat)
    f = wa.shape[1]
    total = None
    for k, w in enumerate((wa, wb)):
        rows = jnp.concatenate([w[lax.rem(pos[3] + j, 4)] for j in range(4)], axis=0)
        part = lax.dot_general(rows, cat[k], (((1,), (1,)), ((), ())), preferred_element_type=jnp.float32)
        total = part if total is None else total + part
    for j in range(4):
        outs[j][...] = total[j * f : j * f + f].astype(jnp.bfloat16)


def hidden_grad_call(pos, wa, wb, sets):
    n, f, d = wa.shape
    t = 512
    specs, args = set_blocks(sets, (0, 1))
    wspec = pl.BlockSpec((n, f, d), lambda i, p: (0, 0, 0))
    return pl.pallas_call(
        hidden_grad_kernel,
        grid_spec=pltpu.PrefetchScalarGridSpec(
            num_scalar_prefetch=1,
            grid=(1,),
            in_specs=[wspec, wspec] + specs,
            out_specs=[pl.BlockSpec(memory_space=pltpu.VMEM)] * n,
            scratch_shapes=[pltpu.VMEM((2, t, d), jnp.bfloat16)],
        ),
        out_shape=[pltpu.VMEM((f, t), jnp.bfloat16)] * n,
        compiler_params=pltpu.CompilerParams(vmem_limit_bytes=24 * 1024 * 1024),
        cost_estimate=pl.CostEstimate(flops=4 * n * f * t * d, bytes_accessed=7 * 1024 * 1024, transcendentals=0),
    )(pos, wa, wb, *args)


def shards(grad_out, gate_pre, up_pre, down_weight):
    depth, row, col = lax.axis_index("depth"), lax.axis_index("row"), lax.axis_index("col")
    pos = jnp.stack([depth % 2, 1 - depth % 2, col % 4, row, depth // 2]).astype(jnp.int32)

    wa = lax.all_to_all(columns_call(pos, down_weight), "row", 0, 0)
    wb = other_core(wa)

    set0 = lax.all_gather(grad_out, "col", axis=0, axis_index_groups=ZG)
    set2 = (from_col(set0[0::2], 2), from_col(set0[1::2], -2))
    set1 = from_col(set0, 1)
    set3 = from_col(set0, -1)
    sets = (set0, set1, set2, set3)

    hid = lax.all_gather(hidden_call(gate_pre.T, up_pre.T, set0), "row", axis=0)

    away = partial_call(pos, 1, hid, sets)
    both = partial_call(pos, 0, hid, sets, other_core(away))
    terms = hidden_grad_call(pos, wa, wb, sets)
    parts = [both[0]]
    for j in (1, 3, 2):
        parts.append(lax.ppermute(both[j], "depth", [(i, (i + 2 * j) % 8) for i in range(8)]))
    perm = []
    for y in range(4):
        for c in range(2):
            for x in range(4):
                perm.append(((2 * y + c) * 4 + x, (2 * x + c) * 4 + (y - x) % 4))
    grad_down = lax.ppermute(sum_call(parts, terms[0]), ("depth", "row"), perm)

    gate = gate_pre.T.astype(jnp.float32)
    upval = up_pre.T.astype(jnp.float32)
    sigma = jax.nn.sigmoid(gate)
    active = gate * sigma
    grad_hidden = terms[0].astype(jnp.float32)
    for j in (1, 3, 2):
        got = lax.ppermute(terms[j], "row", [(i, (i + j) % 4) for i in range(4)])
        grad_hidden = grad_hidden + got.astype(jnp.float32)
    grad_up = (grad_hidden * active).astype(jnp.bfloat16)
    grad_gate = (grad_hidden * upval * sigma * (1.0 + gate * (1.0 - sigma))).astype(jnp.bfloat16)
    return (grad_gate.T, grad_up.T, grad_down)


def solution(mesh):
    in_specs = (
        P("depth", ("row", "col")),
        P("depth", ("row", "col")),
        P("depth", ("row", "col")),
        P(("row", "col"), None),
    )
    out_specs = (P("depth", ("row", "col")), P("depth", ("row", "col")), P(("row", "col"), "depth"))
    return jax.shard_map(shards, mesh=mesh, in_specs=in_specs, out_specs=out_specs, check_vma=False)
```

```python
import jax
import jax.numpy as jnp
from jax import lax
from jax.experimental import pallas as pl
from jax.experimental.pallas import tpu as pltpu
from jax.sharding import PartitionSpec as P

ZG = [[g + 4 * j for j in range(4)] for g in range(4)]

def from_col(a, k):
    return lax.ppermute(a, "col", [((i + k) % 16, i) for i in range(16)])


def other_core(a):
    return lax.ppermute(a, "depth", [(i, i ^ 1) for i in range(8)])


def columns_kernel(pos, w, out, sems):
    d = out.shape[2]
    copies = [
        pltpu.make_async_copy(w.at[:, pl.ds(pl.multiple_of((2 * i + pos[0]) * d, d), d)], out.at[i], sems.at[i])
        for i in range(4)
    ]
    for c in copies:
        c.start()
    for c in copies:
        c.wait()


def columns_call(pos, w):
    f, d = w.shape
    return pl.pallas_call(
        columns_kernel,
        grid_spec=pltpu.PrefetchScalarGridSpec(
            num_scalar_prefetch=1,
            grid=(1,),
            in_specs=[pl.BlockSpec(memory_space=pltpu.HBM)],
            out_specs=pl.BlockSpec((4, f, d // 8), lambda g, p: (0, 0, 0)),
            scratch_shapes=[pltpu.SemaphoreType.DMA((4,))],
        ),
        out_shape=jax.ShapeDtypeStruct((4, f, d // 8), jnp.bfloat16),
        compiler_params=pltpu.CompilerParams(vmem_limit_bytes=12 * 1024 * 1024),
        cost_estimate=pl.CostEstimate(flops=0, bytes_accessed=2 * f * d, transcendentals=0),
    )(pos, w)


def hidden_kernel(gate, up, *refs):
    out = refs[-1]
    g = gate[...].astype(jnp.float32)
    out[...] = (g * jax.nn.sigmoid(g) * up[...].astype(jnp.float32)).astype(out.dtype)


def hidden_call(gate, up, *after):
    spec = pl.BlockSpec(gate.shape, lambda i: (0, 0))
    return pl.pallas_call(
        hidden_kernel,
        grid=(1,),
        in_specs=[spec, spec] + [pl.BlockSpec(memory_space=pl.ANY)] * len(after),
        out_specs=spec,
        out_shape=jax.ShapeDtypeStruct(gate.shape, jnp.bfloat16),
        compiler_params=pltpu.CompilerParams(vmem_limit_bytes=8 * 1024 * 1024),
        cost_estimate=pl.CostEstimate(flops=0, bytes_accessed=6 * gate.size, transcendentals=gate.size),
    )(gate, up, *after)


def gather_features(pos, sets, halves, cat):
    s0, s1, s2e, s2o, s3 = sets
    for k, h in enumerate(halves):
        for q in range(2):
            zg = 2 * h + q
            for r, block in enumerate((s0[zg], s1[zg], (s2e, s2o)[q][h], s3[zg])):
                at = pl.multiple_of(q * 512 + lax.rem(pos[2] + r, 4) * 128, 128)
                cat[k, :, pl.ds(at, 128)] = block


def rows_of(pos, hid, j):
    return hid[lax.rem(pos[4] + 4 + j - pos[3], 4)]


def away_kernel(pos, hid, s0, s1, s2e, s2o, s3, out, cat):
    gather_features(pos, (s0, s1, s2e, s2o, s3), (pos[1],), cat)
    for j in range(4):
        p = jnp.dot(rows_of(pos, hid, j), cat[0], preferred_element_type=jnp.float32)
        out[j] = (p * (1.0 / 64.0)).astype(out.dtype)


def both_kernel(pos, hid, s0, s1, s2e, s2o, s3, got, o0, o1, o2, o3, cat):
    gather_features(pos, (s0, s1, s2e, s2o, s3), (pos[0],), cat)
    for j, out in enumerate((o0, o1, o2, o3)):
        p = jnp.dot(rows_of(pos, hid, j), cat[0], preferred_element_type=jnp.float32)
        out[...] = (p * (1.0 / 64.0) + got[j].astype(jnp.float32)).astype(out.dtype)


def on_core(kernel, pos, args, out_shape, scratch, flops):
    vmem = pl.BlockSpec(memory_space=pltpu.VMEM)
    return pl.pallas_call(
        kernel,
        in_specs=[pl.BlockSpec(memory_space=pltpu.SMEM)] + [vmem] * len(args),
        out_specs=jax.tree.map(lambda _: vmem, out_shape, is_leaf=lambda o: not isinstance(o, list)),
        out_shape=out_shape,
        scratch_shapes=[scratch],
        compiler_params=pltpu.CompilerParams(vmem_limit_bytes=24 * 1024 * 1024),
        cost_estimate=pl.CostEstimate(flops=flops, bytes_accessed=5 * 1024 * 1024, transcendentals=0),
    )(pos, *args)


def partial_call(pos, hid, sets, got=None):
    n, f, t = hid.shape
    cat = pltpu.VMEM((1, t, 1024), jnp.bfloat16)
    flops = 2 * n * f * t * 1024
    if got is None:
        return on_core(away_kernel, pos, (hid, *sets), pltpu.VMEM((n, f, 1024), jnp.bfloat16), cat, flops)
    outs = [pltpu.VMEM((f, 1024), jnp.bfloat16)] * n
    return on_core(both_kernel, pos, (hid, *sets, got), outs, cat, flops)


def tie_kernel(a, after, out):
    pass


def tie(a, after):
    any_space = pl.BlockSpec(memory_space=pl.ANY)
    return pl.pallas_call(
        tie_kernel,
        in_specs=[any_space, any_space],
        out_specs=any_space,
        out_shape=jax.ShapeDtypeStruct(a.shape, a.dtype),
        input_output_aliases={0: 0},
        compiler_params=pltpu.CompilerParams(vmem_limit_bytes=1024 * 1024),
    )(a, after)


def sum_kernel(a, b, c, d, after, out):
    total = a[...].astype(jnp.float32) + b[...].astype(jnp.float32)
    out[...] = (total + c[...].astype(jnp.float32) + d[...].astype(jnp.float32)).astype(out.dtype)


def sum_call(parts, after):
    f, d = parts[0].shape
    return pl.pallas_call(
        sum_kernel,
        in_specs=[pl.BlockSpec(memory_space=pltpu.VMEM)] * 4 + [pl.BlockSpec(memory_space=pl.ANY)],
        out_specs=pl.BlockSpec(memory_space=pltpu.VMEM),
        out_shape=pltpu.VMEM((f, d), jnp.bfloat16),
        compiler_params=pltpu.CompilerParams(vmem_limit_bytes=8 * 1024 * 1024),
        cost_estimate=pl.CostEstimate(flops=3 * f * d, bytes_accessed=10 * f * d, transcendentals=0),
    )(*parts, after)


def hidden_grad_kernel(pos, wa, wb, s0, s1, s2e, s2o, s3, o0, o1, o2, o3, cat):
    gather_features(pos, (s0, s1, s2e, s2o, s3), (pos[0], pos[1]), cat)
    f = wa.shape[1]
    total = None
    for k, w in enumerate((wa, wb)):
        rows = jnp.concatenate([w[lax.rem(pos[3] + j, 4)] for j in range(4)], axis=0)
        part = lax.dot_general(rows, cat[k], (((1,), (1,)), ((), ())), preferred_element_type=jnp.float32)
        total = part if total is None else total + part
    for j, out in enumerate((o0, o1, o2, o3)):
        out[...] = total[j * f : j * f + f].astype(out.dtype)


def hidden_grad_call(pos, wa, wb, sets):
    n, f, d = wa.shape
    t = sets[0].shape[1]
    outs = [pltpu.VMEM((f, t), jnp.bfloat16)] * n
    cat = pltpu.VMEM((2, t, d), jnp.bfloat16)
    return on_core(hidden_grad_kernel, pos, (wa, wb, *sets), outs, cat, 4 * n * f * t * d)


def shards(grad_out, gate_pre, up_pre, down_weight):
    depth, row, col = lax.axis_index("depth"), lax.axis_index("row"), lax.axis_index("col")
    pos = jnp.stack([depth % 2, 1 - depth % 2, col % 4, row, depth // 2]).astype(jnp.int32)

    wa = lax.all_to_all(columns_call(pos, down_weight), "row", 0, 0)
    set0 = tie(lax.all_gather(grad_out, "col", axis=0, axis_index_groups=ZG), wa)
    set2 = (from_col(set0[0::2], 2), from_col(set0[1::2], -2))
    set1 = from_col(set0, 1)
    set3 = from_col(set0, -1)
    sets = (set0, set1, *set2, set3)

    hid = lax.all_gather(hidden_call(gate_pre.T, up_pre.T, set0), "row", axis=0)

    away = partial_call(pos, hid, sets)
    both = partial_call(pos, hid, sets, other_core(away))
    terms = hidden_grad_call(pos, wa, other_core(wa), sets)
    parts = [both[0]]
    for j in (1, 3, 2):
        parts.append(lax.ppermute(both[j], "depth", [(i, (i + 2 * j) % 8) for i in range(8)]))
    perm = []
    for y in range(4):
        for c in range(2):
            for x in range(4):
                perm.append(((2 * y + c) * 4 + x, (2 * x + c) * 4 + (y - x) % 4))
    grad_down = lax.ppermute(sum_call(parts, terms[0]), ("depth", "row"), perm)

    gate = gate_pre.T.astype(jnp.float32)
    upval = up_pre.T.astype(jnp.float32)
    sigma = jax.nn.sigmoid(gate)
    active = gate * sigma
    grad_hidden = terms[0].astype(jnp.float32)
    for j in (1, 3, 2):
        got = lax.ppermute(terms[j], "row", [(i, (i + j) % 4) for i in range(4)])
        grad_hidden = grad_hidden + got.astype(jnp.float32)
    grad_up = (grad_hidden * active).astype(jnp.bfloat16)
    grad_gate = (grad_hidden * upval * sigma * (1.0 + gate * (1.0 - sigma))).astype(jnp.bfloat16)
    return (grad_gate.T, grad_up.T, grad_down)


def solution(mesh):
    in_specs = (
        P("depth", ("row", "col")),
        P("depth", ("row", "col")),
        P("depth", ("row", "col")),
        P(("row", "col"), None),
    )
    out_specs = (P("depth", ("row", "col")), P("depth", ("row", "col")), P(("row", "col"), "depth"))
    return jax.shard_map(shards, mesh=mesh, in_specs=in_specs, out_specs=out_specs, check_vma=False)
```

```python
import jax
import jax.numpy as jnp
from jax import lax
from jax.experimental import pallas as pl
from jax.experimental.pallas import tpu as pltpu
from jax.sharding import PartitionSpec as P

ZG = [[g + 4 * j for j in range(4)] for g in range(4)]

def from_col(a, k):
    return lax.ppermute(a, "col", [((i + k) % 16, i) for i in range(16)])


def other_core(a):
    return lax.ppermute(a, "depth", [(i, i ^ 1) for i in range(8)])


def columns_kernel(pos, w, out, held, sems):
    n, _, d = out.shape
    ins, outs = [], []
    for i in range(n):
        at = pl.multiple_of((2 * i + pos[0]) * d, d)
        ins.append(pltpu.make_async_copy(w.at[:, pl.ds(at, d)], held.at[i], sems.at[0, i]))
        outs.append(pltpu.make_async_copy(held.at[i], out.at[i], sems.at[1, i]))
        ins[i].start()
    for i in range(n):
        ins[i].wait()
        outs[i].start()
    for i in range(n):
        outs[i].wait()


def columns_call(pos, w):
    f, d = w.shape
    return pl.pallas_call(
        columns_kernel,
        in_specs=[pl.BlockSpec(memory_space=pltpu.SMEM), pl.BlockSpec(memory_space=pltpu.HBM)],
        out_specs=pl.BlockSpec(memory_space=pltpu.HBM),
        out_shape=pltpu.HBM((4, f, d // 8), jnp.bfloat16),
        scratch_shapes=[pltpu.VMEM((4, f, d // 8), jnp.bfloat16), pltpu.SemaphoreType.DMA((2, 4))],
        compiler_params=pltpu.CompilerParams(vmem_limit_bytes=12 * 1024 * 1024),
        cost_estimate=pl.CostEstimate(flops=0, bytes_accessed=2 * f * d, transcendentals=0),
    )(pos, pltpu.with_memory_space_constraint(w, pltpu.HBM))


def hidden_kernel(gate, up, *refs):
    out = refs[-1]
    g = gate[...].astype(jnp.float32)
    out[...] = (g * jax.nn.sigmoid(g) * up[...].astype(jnp.float32)).astype(out.dtype)


def hidden_call(gate, up, *after):
    spec = pl.BlockSpec(gate.shape, lambda i: (0, 0))
    return pl.pallas_call(
        hidden_kernel,
        grid=(1,),
        in_specs=[spec, spec] + [pl.BlockSpec(memory_space=pl.ANY)] * len(after),
        out_specs=spec,
        out_shape=jax.ShapeDtypeStruct(gate.shape, jnp.bfloat16),
        compiler_params=pltpu.CompilerParams(vmem_limit_bytes=8 * 1024 * 1024),
        cost_estimate=pl.CostEstimate(flops=0, bytes_accessed=6 * gate.size, transcendentals=gate.size),
    )(gate, up, *after)


def gather_features(pos, sets, halves, cat):
    s0, s1, s2e, s2o, s3 = sets
    for k, h in enumerate(halves):
        for q in range(2):
            zg = 2 * h + q
            for r, block in enumerate((s0[zg], s1[zg], (s2e, s2o)[q][h], s3[zg])):
                at = pl.multiple_of(q * 512 + lax.rem(pos[2] + r, 4) * 128, 128)
                cat[k, :, pl.ds(at, 128)] = block


def rows_of(pos, hid, j):
    return hid[lax.rem(pos[4] + 4 + j - pos[3], 4)]


def away_kernel(pos, hid, s0, s1, s2e, s2o, s3, out, cat):
    gather_features(pos, (s0, s1, s2e, s2o, s3), (pos[1],), cat)
    for j in range(4):
        p = jnp.dot(rows_of(pos, hid, j), cat[0], preferred_element_type=jnp.float32)
        out[j] = (p * (1.0 / 64.0)).astype(out.dtype)


def both_kernel(pos, hid, s0, s1, s2e, s2o, s3, got, o0, o1, o2, o3, cat):
    gather_features(pos, (s0, s1, s2e, s2o, s3), (pos[0],), cat)
    for j, out in enumerate((o0, o1, o2, o3)):
        p = jnp.dot(rows_of(pos, hid, j), cat[0], preferred_element_type=jnp.float32)
        out[...] = (p * (1.0 / 64.0) + got[j].astype(jnp.float32)).astype(out.dtype)


def on_core(kernel, pos, args, out_shape, scratch, flops):
    vmem = pl.BlockSpec(memory_space=pltpu.VMEM)
    return pl.pallas_call(
        kernel,
        in_specs=[pl.BlockSpec(memory_space=pltpu.SMEM)] + [vmem] * len(args),
        out_specs=jax.tree.map(lambda _: vmem, out_shape, is_leaf=lambda o: not isinstance(o, list)),
        out_shape=out_shape,
        scratch_shapes=[scratch],
        compiler_params=pltpu.CompilerParams(vmem_limit_bytes=24 * 1024 * 1024),
        cost_estimate=pl.CostEstimate(flops=flops, bytes_accessed=5 * 1024 * 1024, transcendentals=0),
    )(pos, *args)


def partial_call(pos, hid, sets, got=None):
    n, f, t = hid.shape
    cat = pltpu.VMEM((1, t, 1024), jnp.bfloat16)
    flops = 2 * n * f * t * 1024
    if got is None:
        return on_core(away_kernel, pos, (hid, *sets), pltpu.VMEM((n, f, 1024), jnp.bfloat16), cat, flops)
    outs = [pltpu.VMEM((f, 1024), jnp.bfloat16)] * n
    return on_core(both_kernel, pos, (hid, *sets, got), outs, cat, flops)


def tie_kernel(a, after, out):
    pass


def tie(a, after):
    any_space = pl.BlockSpec(memory_space=pl.ANY)
    return pl.pallas_call(
        tie_kernel,
        in_specs=[any_space, any_space],
        out_specs=any_space,
        out_shape=jax.ShapeDtypeStruct(a.shape, a.dtype),
        input_output_aliases={0: 0},
        compiler_params=pltpu.CompilerParams(vmem_limit_bytes=1024 * 1024),
    )(a, after)


def sum_kernel(a, b, c, d, after, out):
    total = a[...].astype(jnp.float32) + b[...].astype(jnp.float32)
    out[...] = (total + c[...].astype(jnp.float32) + d[...].astype(jnp.float32)).astype(out.dtype)


def sum_call(parts, after):
    f, d = parts[0].shape
    return pl.pallas_call(
        sum_kernel,
        in_specs=[pl.BlockSpec(memory_space=pltpu.VMEM)] * 4 + [pl.BlockSpec(memory_space=pl.ANY)],
        out_specs=pl.BlockSpec(memory_space=pltpu.VMEM),
        out_shape=pltpu.VMEM((f, d), jnp.bfloat16),
        compiler_params=pltpu.CompilerParams(vmem_limit_bytes=8 * 1024 * 1024),
        cost_estimate=pl.CostEstimate(flops=3 * f * d, bytes_accessed=10 * f * d, transcendentals=0),
    )(*parts, after)


def hidden_grad_kernel(pos, wa, wb, s0, s1, s2e, s2o, s3, o0, o1, o2, o3, cat):
    gather_features(pos, (s0, s1, s2e, s2o, s3), (pos[0], pos[1]), cat)
    f = wa.shape[1]
    total = None
    for k, w in enumerate((wa, wb)):
        rows = jnp.concatenate([w[lax.rem(pos[3] + j, 4)] for j in range(4)], axis=0)
        part = lax.dot_general(rows, cat[k], (((1,), (1,)), ((), ())), preferred_element_type=jnp.float32)
        total = part if total is None else total + part
    for j, out in enumerate((o0, o1, o2, o3)):
        out[...] = total[j * f : j * f + f].astype(out.dtype)


def hidden_grad_call(pos, wa, wb, sets):
    n, f, d = wa.shape
    t = sets[0].shape[1]
    outs = [pltpu.VMEM((f, t), jnp.bfloat16)] * n
    cat = pltpu.VMEM((2, t, d), jnp.bfloat16)
    return on_core(hidden_grad_kernel, pos, (wa, wb, *sets), outs, cat, 4 * n * f * t * d)


def shards(grad_out, gate_pre, up_pre, down_weight):
    depth, row, col = lax.axis_index("depth"), lax.axis_index("row"), lax.axis_index("col")
    pos = jnp.stack([depth % 2, 1 - depth % 2, col % 4, row, depth // 2]).astype(jnp.int32)

    wa = lax.all_to_all(columns_call(pos, down_weight), "row", 0, 0)
    set0 = tie(lax.all_gather(grad_out, "col", axis=0, axis_index_groups=ZG), wa)
    set2 = (from_col(set0[0::2], 2), from_col(set0[1::2], -2))
    set1 = from_col(set0, 1)
    set3 = from_col(set0, -1)
    sets = (set0, set1, *set2, set3)

    hid = lax.all_gather(hidden_call(gate_pre.T, up_pre.T, set0), "row", axis=0)

    away = partial_call(pos, hid, sets)
    both = partial_call(pos, hid, sets, other_core(away))
    terms = hidden_grad_call(pos, wa, other_core(wa), sets)
    parts = [both[0]]
    for j in (1, 3, 2):
        parts.append(lax.ppermute(both[j], "depth", [(i, (i + 2 * j) % 8) for i in range(8)]))
    perm = []
    for y in range(4):
        for c in range(2):
            for x in range(4):
                perm.append(((2 * y + c) * 4 + x, (2 * x + c) * 4 + (y - x) % 4))
    grad_down = lax.ppermute(sum_call(parts, terms[0]), ("depth", "row"), perm)

    gate = gate_pre.T.astype(jnp.float32)
    upval = up_pre.T.astype(jnp.float32)
    sigma = jax.nn.sigmoid(gate)
    active = gate * sigma
    grad_hidden = terms[0].astype(jnp.float32)
    for j in (1, 3, 2):
        got = lax.ppermute(terms[j], "row", [(i, (i + j) % 4) for i in range(4)])
        grad_hidden = grad_hidden + got.astype(jnp.float32)
    grad_up = (grad_hidden * active).astype(jnp.bfloat16)
    grad_gate = (grad_hidden * upval * sigma * (1.0 + gate * (1.0 - sigma))).astype(jnp.bfloat16)
    return (grad_gate.T, grad_up.T, grad_down)


def solution(mesh):
    in_specs = (
        P("depth", ("row", "col")),
        P("depth", ("row", "col")),
        P("depth", ("row", "col")),
        P(("row", "col"), None),
    )
    out_specs = (P("depth", ("row", "col")), P("depth", ("row", "col")), P(("row", "col"), "depth"))
    return jax.shard_map(shards, mesh=mesh, in_specs=in_specs, out_specs=out_specs, check_vma=False)
```
